32 devices in a mesh: groups: 2 (over y), blk: 8 (over z, x), narrow: 2 (over core).
Axes of the slice: x: 2, y: 2, z: 4, core: 2. Of those that a mesh axis runs over, the one named last changes fastest.
Arguments:
- tokens: bfloat16 [256, 8192], P(('groups', 'blk'), 'narrow'), parts along dimension 0, may hold values from -6 to 6
- gate_weight: bfloat16 [8192, 24576], P('narrow', 'blk'), may hold values from -0.09375 to 0.09375
- up_weight: bfloat16 [8192, 24576], P('narrow', 'blk'), may hold values from -0.09375 to 0.09375
- gate_mask: int32 [64, 192], P('narrow', 'blk'), may hold values from 0 to 1, as said below
- up_mask: int32 [64, 192], P('narrow', 'blk'), may hold values from 0 to 1, as said below
- down_weight: bfloat16 [24576, 8192], P('blk', 'narrow'), may hold values from -0.0546875 to 0.0546875
- down_mask: int32 [192, 64], P('blk', 'narrow'), may hold values from 0 to 1, as said below
Outputs:
- mixed: bfloat16 [256, 8192], P(('groups', 'blk'), 'narrow'), parts along dimension 0
The draws below stay inside these ranges and needn't reach their ends.
There are 2 independent parts, one for each index of `groups`. The reference program is written for one: setup_inputs(seed, part) draws one part's arguments, and reference() takes and returns one part's arrays. A program takes and returns all parts, laid end to end along the dimension named above; an argument that names none is the same for every part. Nothing has to cross between parts.
Inputs may be any that keep to these rules, and one draw needn't show every extreme that they name: `gate_mask`: entries are 0 or 1; the share kept may differ from one column of blocks (gate, up) or row of blocks (down) to the next. `up_mask`: as gate_mask. `down_mask`: as gate_mask.
All inputs are finite; a program needn't handle non-finite values.
Results may differ from the reference program's by a relative error of at most 0.0049.
Values may be sent and summed in bfloat16 or wider, within the bound.
A program may use at most 320 MiB of HBM per device.

```python
import jax
import jax.numpy as jnp

D = 8192
FF = 24576
BLOCK = 128
TOKENS = 128


def block_mask(key, rows, cols, along_rows):
    rate_key, entry_key = jax.random.split(key)
    if along_rows:
        rates = jax.random.randint(rate_key, (rows, 1), 1, 4)
    else:
        rates = jax.random.randint(rate_key, (1, cols), 1, 4)
    entries = jax.random.randint(entry_key, (rows, cols), 0, 4)
    return (entries < rates).astype(jnp.int32)


def draw_gate_mask(key, part):
    key = jax.random.fold_in(key, 11)
    return block_mask(key, D // BLOCK, FF // BLOCK, False)


def draw_up_mask(key, part):
    key = jax.random.fold_in(key, 23)
    return block_mask(key, D // BLOCK, FF // BLOCK, False)


def draw_down_mask(key, part):
    key = jax.random.fold_in(key, 37)
    return block_mask(key, FF // BLOCK, D // BLOCK, True)


def level_of(key, extent, cuts, low, high):
    level, own = 1.0, jax.random.fold_in(key, 6)
    for dim, parts in cuts:
        draws = jnp.exp(jax.random.uniform(jax.random.fold_in(own, dim), (parts,), jnp.float32, low / len(cuts), high / len(cuts)))
        level = level * jnp.repeat(draws, extent[dim] // parts).reshape([-1 if axis == dim else 1 for axis in range(len(extent))])
    return level


def scatter_about(own_key, shape, deviation, limit, shards=(), held_as=jnp.bfloat16):
    values = deviation * jax.random.normal(own_key, shape, jnp.float32)
    if shards:
        values = values * level_of(own_key, shape, shards, -0.22, 0.18)
    return jnp.clip(values, -limit, limit).astype(held_as)


def setup_inputs(seed: int = 0, part: int = 0) -> dict:
    arg_keys = jax.random.split(jax.random.key(seed), 8)
    part_splits = jax.random.split(jax.random.fold_in(arg_keys[7], part), 8)
    return {
        "tokens": scatter_about(part_splits[0], (TOKENS, D), 1.0, 6.0, ((0, 8), (1, 2))),
        "gate_weight": scatter_about(arg_keys[1], (D, FF), (D // 2) ** -0.5, 0.09375, ((0, 2), (1, 8))),
        "up_weight": scatter_about(arg_keys[2], (D, FF), (D // 2) ** -0.5, 0.09375, ((0, 2), (1, 8))),
        "gate_mask": draw_gate_mask(jax.random.fold_in(arg_keys[7], 71), part),
        "up_mask": draw_up_mask(jax.random.fold_in(arg_keys[7], 71), part),
        "down_weight": scatter_about(arg_keys[5], (FF, D), (FF // 2) ** -0.5, 0.0546875, ((0, 8), (1, 2))),
        "down_mask": draw_down_mask(jax.random.fold_in(arg_keys[7], 71), part),
    }


def expand(weight, mask):
    rows, cols = mask.shape
    tiled = weight.reshape(rows, BLOCK, cols, BLOCK) * mask[:, None, :, None].astype(weight.dtype)
    return tiled.reshape(weight.shape)


def reference(tokens, gate_weight, up_weight, gate_mask, up_mask, down_weight, down_mask):
    gate = jnp.dot(tokens, expand(gate_weight, gate_mask), preferred_element_type=jnp.float32)
    up = jnp.dot(tokens, expand(up_weight, up_mask), preferred_element_type=jnp.float32)
    hidden = (jax.nn.silu(gate) * up).astype(jnp.bfloat16)
    mixed = jnp.dot(hidden, expand(down_weight, down_mask), preferred_element_type=jnp.float32)
    return mixed.astype(jnp.bfloat16)
```

```python
import functools

import jax
import jax.numpy as jnp
from jax import lax
from jax.experimental import pallas as pl
from jax.experimental.pallas import tpu as pltpu
from jax.sharding import PartitionSpec as P

MESH = pl.DeviceIdType.MESH
BF = jnp.bfloat16
F32 = jnp.float32


def kernel(
    cfg,
    tok, gw, uw, gm, um, dw, dm, out,
    x, wg, wu, wd, gx, ux, dx, accg, accu, exs, exr, hid, pt, sx, rx, own, sa, ra, own2,
    g_sem, u_sem, d_sem, t_sem,
    a_send, a_recv, f_send, f_recv, e_send, e_recv, x_send, x_recv, z_send, z_recv,
):
    A, B, TR, M, MB, K, F, D, C, KC, S, KS, SD, TC, TN, BS = cfg
    blk, nar = lax.axis_index("blk"), lax.axis_index("narrow")
    a, b = lax.div(blk, B), lax.rem(blk, B)
    GR = A * TR
    NS, NT, T, SPC = K // KS, F // TN, D // TC, KC // KS

    def a_peer(d):
        return lax.rem(a + d, A)

    def b_peer(e):
        return lax.rem(b + e, B)

    def slab(s):
        slot = lax.rem(s, S)
        rows = pl.ds(pl.multiple_of(s * KS, KS), KS)
        return (
            pltpu.make_async_copy(gw.at[rows, :], wg.at[slot], g_sem.at[slot]),
            pltpu.make_async_copy(uw.at[rows, :], wu.at[slot], u_sem.at[slot]),
        )

    def down(c):
        slot = lax.rem(c, SD)
        cols = pl.ds(pl.multiple_of(c * TC, TC), TC)
        return pltpu.make_async_copy(dw.at[:, cols], wd.at[slot], d_sem.at[slot])

    p0 = pl.multiple_of((b * A + a) * TR, TR)
    g0 = pl.multiple_of(b * GR, GR)

    def gather(c, d):
        cols = pl.ds(c * KC, KC)
        return pltpu.make_async_remote_copy(
            src_ref=tok.at[:, cols], dst_ref=x.at[pl.ds(p0, TR), cols],
            send_sem=a_send.at[c, d - 1], recv_sem=a_recv.at[c, d - 1],
            device_id={"blk": a_peer(d) * B + b}, device_id_type=MESH)

    def gather_in(c, d):
        cols = pl.ds(c * KC, KC)
        src = lax.rem(a - d + A, A)
        r = pl.multiple_of((b * A + src) * TR, TR)
        return pltpu.make_async_remote_copy(
            src_ref=tok.at[:, cols], dst_ref=x.at[pl.ds(r, TR), cols],
            send_sem=a_send.at[c, d - 1], recv_sem=a_recv.at[c, d - 1],
            device_id={"blk": a_peer(d) * B + b}, device_id_type=MESH)

    def forward(c, e, r):
        cols = pl.ds(c * KC, KC)
        return pltpu.make_async_remote_copy(
            src_ref=x.at[pl.ds(g0, GR), cols], dst_ref=x.at[pl.ds(r, GR), cols],
            send_sem=f_send.at[c, e - 1], recv_sem=f_recv.at[c, e - 1],
            device_id={"blk": a * B + b_peer(e)}, device_id_type=MESH)

    def forward_in(c, e):
        return forward(c, e, pl.multiple_of(lax.rem(b - e + B, B) * GR, GR))

    def exchange(j):
        return pltpu.make_async_remote_copy(
            src_ref=exs.at[j], dst_ref=exr.at[j],
            send_sem=e_send.at[j], recv_sem=e_recv.at[j],
            device_id={"narrow": 1 - nar}, device_id_type=MESH)

    def to_b(c, e):
        r = pl.multiple_of(b_peer(e) * GR, GR)
        return pltpu.make_async_remote_copy(
            src_ref=sx.at[c, pl.ds(r, GR), :], dst_ref=rx.at[c, e - 1],
            send_sem=x_send.at[c, e - 1], recv_sem=x_recv.at[c, e - 1],
            device_id={"blk": a * B + b_peer(e)}, device_id_type=MESH)

    def to_a(c, d):
        r = pl.multiple_of(a_peer(d) * TR, TR)
        return pltpu.make_async_remote_copy(
            src_ref=sa.at[c, pl.ds(r, TR), :], dst_ref=ra.at[c, d - 1],
            send_sem=z_send.at[c, d - 1], recv_sem=z_recv.at[c, d - 1],
            device_id={"blk": a_peer(d) * B + b}, device_id_type=MESH)

    mine = pltpu.make_async_copy(tok, x.at[pl.ds(p0, TR), :], t_sem)
    mine.start()
    for s in range(min(S, NS)):
        for cp in slab(s):
            cp.start()

    barrier = pltpu.get_barrier_semaphore()
    for d in range(1, A):
        pl.semaphore_signal(barrier, inc=1, device_id={"blk": a_peer(d) * B + b}, device_id_type=MESH)
    for e in range(1, B):
        pl.semaphore_signal(barrier, inc=1, device_id={"blk": a * B + b_peer(e)}, device_id_type=MESH)
    pl.semaphore_signal(barrier, inc=1, device_id={"narrow": 1 - nar}, device_id_type=MESH)
    pl.semaphore_wait(barrier, A + B - 1)

    for c in range(C):
        for d in range(1, A):
            gather(c, d).start()

    for mask, spread in ((gm, gx), (um, ux), (dm, dx)):
        m = mask[...].astype(F32)
        for n in range(m.shape[1]):
            spread[:, n * BS:(n + 1) * BS] = jnp.broadcast_to(m[:, n:n + 1], (m.shape[0], BS))
    accg[...] = jnp.zeros_like(accg)
    accu[...] = jnp.zeros_like(accu)

    def relay(c):
        if c == 0:
            mine.wait()
        for d in range(1, A):
            gather_in(c, d).wait_recv()
        for e in range(1, B):
            forward(c, e, g0).start()

    def masked(w, spread, row, cols):
        rows, width = w.shape
        parts = []
        for i in range(rows // BS):
            m = spread[pl.ds(row + i, 1), cols]
            m = jnp.broadcast_to(m, (16, width)).astype(BF)
            wi = w[i * BS:(i + 1) * BS].reshape(BS // 16, 16, width) * m[None]
            parts.append(wi.reshape(BS, width))
        return jnp.concatenate(parts, axis=0)

    KD = 2 * BS

    def product(left, rows, first, w, slot, cols, mcols, spread, row0, depth):
        kd = KD if depth % KD == 0 else BS
        total = None
        for k in range(depth // kd):
            lhs = left[rows, pl.ds(first + k * kd, kd)]
            rhs = masked(w[slot, k * kd:(k + 1) * kd, cols], spread, row0 + k * (kd // BS), mcols)
            part = jnp.dot(lhs, rhs, preferred_element_type=F32)
            total = part if total is None else total + part
        return total

    def slab_step(s, last):
        for cp in slab(s):
            cp.wait()
        slot = lax.rem(s, S)
        first = pl.multiple_of(s * KS, KS)

        def tile(j, _):
            cols = pl.ds(pl.multiple_of(j * TN, TN), TN)
            for i in range(M // MB):
                rows = pl.ds(i * MB, MB)
                for q, (w, spread, acc) in enumerate(((wg, gx, accg), (wu, ux, accu))):
                    t = product(x, rows, first, w, slot, cols, cols, spread, s * (KS // BS), KS)
                    t = t + acc[rows, cols]
                    acc[rows, cols] = t
                    if last:
                        exs[j, q, rows, :] = t.astype(BF)
            if last:
                exchange(j).start()
            return 0

        lax.fori_loop(0, NT, tile, 0)

    relay(0)
    for c in range(C):
        if c + 1 < C:
            relay(c + 1)
        for e in range(1, B):
            forward_in(c, e).wait_recv()
        for i in range(SPC):
            s = c * SPC + i
            slab_step(s, s == NS - 1)
            if s + S < NS:
                for cp in slab(s + S):
                    cp.start()
            else:
                n = s + S - NS
                lo, hi = n * SD // min(S, NS), (n + 1) * SD // min(S, NS)
                for t in range(lo, min(hi, T)):
                    down(t).start()

    def finish(j, _):
        exchange(j).wait_recv()
        cols = pl.ds(pl.multiple_of(j * TN, TN), TN)
        for i in range(M // MB):
            rows = pl.ds(i * MB, MB)
            g = accg[rows, cols] + exr[j, 0, rows, :].astype(F32)
            u = accu[rows, cols] + exr[j, 1, rows, :].astype(F32)
            hid[rows, cols] = (g / (1.0 + jnp.exp(-g)) * u).astype(BF)
        return 0

    lax.fori_loop(0, NT, finish, 0)

    def step(c, _):
        @pl.when(c < T)
        def _():
            down(c).wait()
            slot = lax.rem(c, SD)
            for i in range(M // MB):
                rows = pl.ds(i * MB, MB)

                def part(h, _):
                    cols = pl.ds(pl.multiple_of(h * TN, TN), TN)
                    mcols = pl.ds(pl.multiple_of(c * TC + h * TN, TN), TN)
                    t = product(hid, rows, 0, wd, slot, cols, mcols, dx, 0, F)
                    pt[rows, cols] = t
                    sx[c, rows, cols] = t.astype(BF)
                    return 0

                lax.fori_loop(0, TC // TN, part, 0)
            for e in range(1, B):
                to_b(c, e).start()
            own[c] = pt[pl.ds(g0, GR), :]

            @pl.when(c + SD < T)
            def _():
                down(c + SD).start()

        @pl.when(jnp.logical_and(c >= 1, c <= T))
        def _():
            q = c - 1
            for e in range(1, B):
                to_b(q, e).wait_recv()
            t = own[q]
            for e in range(1, B):
                t = t + rx[q, e - 1].astype(F32)
            own[q] = t
            sa[q] = t.astype(BF)
            for d in range(1, A):
                to_a(q, d).start()
            own2[q] = own[q, pl.ds(pl.multiple_of(a * TR, TR), TR), :]

        @pl.when(c >= 2)
        def _():
            q = c - 2
            for d in range(1, A):
                to_a(q, d).wait_recv()
            t = own2[q]
            for d in range(1, A):
                t = t + ra[q, d - 1].astype(F32)
            out[:, pl.ds(pl.multiple_of(q * TC, TC), TC)] = t.astype(BF)

        return 0

    lax.fori_loop(0, T + 2, step, 0)

    for c in range(C):
        for d in range(1, A):
            gather(c, d).wait_send()
        for e in range(1, B):
            forward(c, e, g0).wait_send()

    def sent(j, _):
        exchange(j).wait_send()
        return 0

    lax.fori_loop(0, NT, sent, 0)

    def sent2(c, _):
        for e in range(1, B):
            to_b(c, e).wait_send()
        for d in range(1, A):
            to_a(c, d).wait_send()
        return 0

    lax.fori_loop(0, T, sent2, 0)


def local(nb, tokens, gate_weight, up_weight, gate_mask, up_mask, down_weight, down_mask):
    TR, K = tokens.shape
    F, D = down_weight.shape
    BS = K // gate_mask.shape[0]
    A = 4 if nb % 4 == 0 else 1
    B = nb // A
    M = TR * nb
    MB = min(M, 128)
    C = 4
    KC = K // C
    KS = KC // 2
    S = 5
    SD = 4
    TC = min(D, 512)
    TN = 256 if F % 256 == 0 else BS
    NT, T = F // TN, D // TC
    GR = A * TR
    cfg = (A, B, TR, M, MB, K, F, D, C, KC, S, KS, SD, TC, TN, BS)
    dma = pltpu.SemaphoreType.DMA
    hbm = pl.BlockSpec(memory_space=pl.ANY)
    vmem = pl.BlockSpec(memory_space=pltpu.VMEM)
    return pl.pallas_call(
        functools.partial(kernel, cfg),
        out_shape=jax.ShapeDtypeStruct((TR, D), BF),
        in_specs=[hbm, hbm, hbm, vmem, vmem, hbm, vmem],
        out_specs=vmem,
        scratch_shapes=[
            pltpu.VMEM((M, K), BF),
            pltpu.VMEM((S, KS, F), BF),
            pltpu.VMEM((S, KS, F), BF),
            pltpu.VMEM((SD, F, TC), BF),
            pltpu.VMEM((K // BS, F), F32),
            pltpu.VMEM((K // BS, F), F32),
            pltpu.VMEM((F // BS, D), F32),
            pltpu.VMEM((M, F), F32),
            pltpu.VMEM((M, F), F32),
            pltpu.VMEM((NT, 2, M, TN), BF),
            pltpu.VMEM((NT, 2, M, TN), BF),
            pltpu.VMEM((M, F), BF),
            pltpu.VMEM((M, TC), F32),
            pltpu.VMEM((T, M, TC), BF),
            pltpu.VMEM((T, max(B - 1, 1), GR, TC), BF),
            pltpu.VMEM((T, GR, TC), F32),
            pltpu.VMEM((T, GR, TC), BF),
            pltpu.VMEM((T, max(A - 1, 1), TR, TC), BF),
            pltpu.VMEM((T, TR, TC), F32),
            dma((S,)), dma((S,)), dma((SD,)), dma(()),
            dma((C, max(A - 1, 1))), dma((C, max(A - 1, 1))),
            dma((C, max(B - 1, 1))), dma((C, max(B - 1, 1))),
            dma((NT,)), dma((NT,)),
            dma((T, max(B - 1, 1))), dma((T, max(B - 1, 1))),
            dma((T, max(A - 1, 1))), dma((T, max(A - 1, 1))),
        ],
        compiler_params=pltpu.CompilerParams(
            collective_id=0, has_side_effects=True, vmem_limit_bytes=62 * 2**20
        ),
        cost_estimate=pl.CostEstimate(
            flops=6 * M * K * F, bytes_accessed=6 * K * F, transcendentals=M * F
        ),
    )(tokens, gate_weight, up_weight, gate_mask, up_mask, down_weight, down_mask)


def solution(mesh):
    in_specs = (
        P(("groups", "blk"), "narrow"),
        P("narrow", "blk"),
        P("narrow", "blk"),
        P("narrow", "blk"),
        P("narrow", "blk"),
        P("blk", "narrow"),
        P("blk", "narrow"),
    )
    out_specs = P(("groups", "blk"), "narrow")
    return jax.shard_map(
        functools.partial(local, mesh.shape["blk"]),
        mesh=mesh, in_specs=in_specs, out_specs=out_specs, check_vma=False,
    )
```

```python
import functools

import jax
import jax.numpy as jnp
from jax import lax
from jax.experimental import pallas as pl
from jax.experimental.pallas import tpu as pltpu
from jax.sharding import PartitionSpec as P

MESH = pl.DeviceIdType.MESH
BF = jnp.bfloat16
F32 = jnp.float32


def kernel(
    cfg,
    tok, gw, uw, gm, um, dw, dm, out,
    x, wg, wu, wd, gx, ux, dx, accg, accu, exs, exr, hid, pt, sx, rx, own, sa, ra, own2,
    g_sem, u_sem, d_sem, t_sem,
    a_send, a_recv, f_send, f_recv, e_send, e_recv, x_send, x_recv, z_send, z_recv,
):
    A, B, TR, M, MB, K, F, D, C, KC, S, KS, SD, TC, TN, BS = cfg
    blk, nar = lax.axis_index("blk"), lax.axis_index("narrow")
    a, b = lax.div(blk, B), lax.rem(blk, B)
    GR = A * TR
    NS, NT, T, SPC = K // KS, F // TN, D // TC, KC // KS

    def a_peer(d):
        return lax.rem(a + d, A)

    def b_peer(e):
        return lax.rem(b + e, B)

    def slab(s):
        slot = lax.rem(s, S)
        rows = pl.ds(pl.multiple_of(s * KS, KS), KS)
        return (
            pltpu.make_async_copy(gw.at[rows, :], wg.at[slot], g_sem.at[slot]),
            pltpu.make_async_copy(uw.at[rows, :], wu.at[slot], u_sem.at[slot]),
        )

    def down(c):
        slot = lax.rem(c, SD)
        cols = pl.ds(pl.multiple_of(c * TC, TC), TC)
        return pltpu.make_async_copy(dw.at[:, cols], wd.at[slot], d_sem.at[slot])

    p0 = pl.multiple_of((b * A + a) * TR, TR)
    g0 = pl.multiple_of(b * GR, GR)

    def gather(c, d):
        cols = pl.ds(c * KC, KC)
        return pltpu.make_async_remote_copy(
            src_ref=tok.at[:, cols], dst_ref=x.at[pl.ds(p0, TR), cols],
            send_sem=a_send.at[c, d - 1], recv_sem=a_recv.at[c, d - 1],
            device_id={"blk": a_peer(d) * B + b}, device_id_type=MESH)

    def gather_in(c, d):
        cols = pl.ds(c * KC, KC)
        src = lax.rem(a - d + A, A)
        r = pl.multiple_of((b * A + src) * TR, TR)
        return pltpu.make_async_remote_copy(
            src_ref=tok.at[:, cols], dst_ref=x.at[pl.ds(r, TR), cols],
            send_sem=a_send.at[c, d - 1], recv_sem=a_recv.at[c, d - 1],
            device_id={"blk": a_peer(d) * B + b}, device_id_type=MESH)

    def forward(c, e, d):
        cols = pl.ds(c * KC, KC)
        r = pl.multiple_of((b * A + lax.rem(a - d + A, A)) * TR, TR)
        dst = x.at[pl.ds(r, TR), cols]
        return pltpu.make_async_remote_copy(
            src_ref=tok.at[:, cols] if d == 0 else dst, dst_ref=dst,
            send_sem=f_send.at[c, e - 1, d], recv_sem=f_recv.at[c, e - 1, d],
            device_id={"blk": a * B + b_peer(e)}, device_id_type=MESH)

    def forward_in(c, e, d):
        cols = pl.ds(c * KC, KC)
        r = pl.multiple_of((lax.rem(b - e + B, B) * A + lax.rem(a - d + A, A)) * TR, TR)
        return pltpu.make_async_remote_copy(
            src_ref=tok.at[:, cols], dst_ref=x.at[pl.ds(r, TR), cols],
            send_sem=f_send.at[c, e - 1, d], recv_sem=f_recv.at[c, e - 1, d],
            device_id={"blk": a * B + b_peer(e)}, device_id_type=MESH)

    def exchange(j):
        return pltpu.make_async_remote_copy(
            src_ref=exs.at[j], dst_ref=exr.at[j],
            send_sem=e_send.at[j], recv_sem=e_recv.at[j],
            device_id={"narrow": 1 - nar}, device_id_type=MESH)

    def to_b(c, e):
        r = pl.multiple_of(b_peer(e) * GR, GR)
        return pltpu.make_async_remote_copy(
            src_ref=sx.at[c, pl.ds(r, GR), :], dst_ref=rx.at[c, e - 1],
            send_sem=x_send.at[c, e - 1], recv_sem=x_recv.at[c, e - 1],
            device_id={"blk": a * B + b_peer(e)}, device_id_type=MESH)

    def to_a(c, d):
        r = pl.multiple_of(a_peer(d) * TR, TR)
        return pltpu.make_async_remote_copy(
            src_ref=sa.at[c, pl.ds(r, TR), :], dst_ref=ra.at[c, d - 1],
            send_sem=z_send.at[c, d - 1], recv_sem=z_recv.at[c, d - 1],
            device_id={"blk": a_peer(d) * B + b}, device_id_type=MESH)

    mine = pltpu.make_async_copy(tok, x.at[pl.ds(p0, TR), :], t_sem)
    mine.start()
    for s in range(min(S, NS)):
        for cp in slab(s):
            cp.start()
    for t in range(min(SD, T)):
        down(t).start()

    barrier = pltpu.get_barrier_semaphore()
    for d in range(1, A):
        pl.semaphore_signal(barrier, inc=1, device_id={"blk": a_peer(d) * B + b}, device_id_type=MESH)
    for e in range(1, B):
        pl.semaphore_signal(barrier, inc=1, device_id={"blk": a * B + b_peer(e)}, device_id_type=MESH)
    pl.semaphore_signal(barrier, inc=1, device_id={"narrow": 1 - nar}, device_id_type=MESH)
    pl.semaphore_wait(barrier, A + B - 1)

    for c in range(C):
        for d in range(1, A):
            gather(c, d).start()
        for e in range(1, B):
            forward(c, e, 0).start()

    for mask, spread in ((gm, gx), (um, ux), (dm, dx)):
        m = mask[...].astype(F32)
        m = m if spread is dx else m.T
        for n in range(m.shape[1]):
            spread[:, n * BS:(n + 1) * BS] = jnp.broadcast_to(m[:, n:n + 1], (m.shape[0], BS))
    accg[...] = jnp.zeros_like(accg)
    accu[...] = jnp.zeros_like(accu)

    def relay(c):
        if c == 0:
            mine.wait()
        for d in range(1, A):
            gather_in(c, d).wait_recv()
            for e in range(1, B):
                forward(c, e, d).start()

    def masked(w, spread, row, cols):
        rows, width = w.shape
        parts = []
        for i in range(rows // BS):
            m = spread[pl.ds(row + i, 1), cols]
            m = jnp.broadcast_to(m, (16, width)).astype(BF)
            wi = w[i * BS:(i + 1) * BS].reshape(BS // 16, 16, width) * m[None]
            parts.append(wi.reshape(BS, width))
        return jnp.concatenate(parts, axis=0)

    KD = 4 * BS
    LX, LZ = 2, 5

    def product(left, rows, first, w, slot, cols, mcols, spread, row0, depth):
        kd = KD if depth % KD == 0 else BS
        total = None
        for k in range(depth // kd):
            lhs = left[rows, pl.ds(first + k * kd, kd)]
            rhs = masked(w[slot, k * kd:(k + 1) * kd, cols], spread, row0 + k * (kd // BS), mcols)
            part = jnp.dot(lhs, rhs, preferred_element_type=F32)
            total = part if total is None else total + part
        return total

    def slab_step(s, last):
        for cp in slab(s):
            cp.wait()
        slot = lax.rem(s, S)
        first = pl.multiple_of(s * KS, KS)

        def tile(j, _):
            cols = pl.ds(pl.multiple_of(j * TN, TN), TN)
            for i in range(M // MB):
                rows = pl.ds(i * MB, MB)
                for q, (w, spread, acc) in enumerate(((wg, gx, accg), (wu, ux, accu))):
                    t = product(x, rows, first, w, slot, cols, cols, spread, s * (KS // BS), KS)
                    t = t + acc[rows, cols]
                    acc[rows, cols] = t
                    if last:
                        exs[j, q, rows, :] = t.astype(BF)
            if last:
                exchange(j).start()
            return 0

        lax.fori_loop(0, NT, tile, 0, unroll=True)

    relay(0)
    relay(1)
    for c in range(C):
        if c + 2 < C:
            relay(c + 2)
        for e in range(1, B):
            for d in range(A):
                forward_in(c, e, d).wait_recv()
        for i in range(SPC):
            s = c * SPC + i
            slab_step(s, s == NS - 1)
            if s + S < NS:
                for cp in slab(s + S):
                    cp.start()

    def finish(j, _):
        exchange(j).wait_recv()
        cols = pl.ds(pl.multiple_of(j * TN, TN), TN)
        for i in range(M // MB):
            rows = pl.ds(i * MB, MB)
            g = accg[rows, cols] + exr[j, 0, rows, :].astype(F32)
            u = accu[rows, cols] + exr[j, 1, rows, :].astype(F32)
            hid[rows, cols] = (g / (1.0 + jnp.exp(-g)) * u).astype(BF)
        return 0

    lax.fori_loop(0, NT, finish, 0, unroll=True)

    def step(c, _):
        @pl.when(c < T)
        def _():
            down(c).wait()
            slot = lax.rem(c, SD)
            for i in range(M // MB):
                rows = pl.ds(i * MB, MB)

                def part(h, _):
                    cols = pl.ds(pl.multiple_of(h * TN, TN), TN)
                    mcols = pl.ds(pl.multiple_of(c * TC + h * TN, TN), TN)
                    t = product(hid, rows, 0, wd, slot, cols, mcols, dx, 0, F)
                    pt[rows, cols] = t
                    sx[c, rows, cols] = t.astype(BF)
                    return 0

                lax.fori_loop(0, TC // TN, part, 0)
            for e in range(1, B):
                to_b(c, e).start()
            own[c] = pt[pl.ds(g0, GR), :]

            @pl.when(c + SD < T)
            def _():
                down(c + SD).start()

        @pl.when(jnp.logical_and(c >= LX, c < T + LX))
        def _():
            q = c - LX
            for e in range(1, B):
                to_b(q, e).wait_recv()
            t = own[q]
            for e in range(1, B):
                t = t + rx[q, e - 1].astype(F32)
            own[q] = t
            sa[q] = t.astype(BF)
            for d in range(1, A):
                to_a(q, d).start()
            own2[q] = own[q, pl.ds(pl.multiple_of(a * TR, TR), TR), :]

        @pl.when(c >= LZ)
        def _():
            q = c - LZ
            for d in range(1, A):
                to_a(q, d).wait_recv()
            t = own2[q]
            for d in range(1, A):
                t = t + ra[q, d - 1].astype(F32)
            out[:, pl.ds(pl.multiple_of(q * TC, TC), TC)] = t.astype(BF)

        return 0

    lax.fori_loop(0, T + LZ, step, 0)

    for c in range(C):
        for d in range(1, A):
            gather(c, d).wait_send()
        for e in range(1, B):
            for d in range(A):
                forward(c, e, d).wait_send()

    def sent(j, _):
        exchange(j).wait_send()
        return 0

    lax.fori_loop(0, NT, sent, 0)

    def sent2(c, _):
        for e in range(1, B):
            to_b(c, e).wait_send()
        for d in range(1, A):
            to_a(c, d).wait_send()
        return 0

    lax.fori_loop(0, T, sent2, 0)


def local(nb, tokens, gate_weight, up_weight, gate_mask, up_mask, down_weight, down_mask):
    TR, K = tokens.shape
    F, D = down_weight.shape
    BS = K // gate_mask.shape[0]
    A = 4 if nb % 4 == 0 else 1
    B = nb // A
    M = TR * nb
    MB = min(M, 128)
    C = 8
    KC = K // C
    KS = KC
    S = 5
    SD = 4
    TC = min(D, 512)
    TN = 512 if F % 512 == 0 else BS
    NT, T = F // TN, D // TC
    GR = A * TR
    cfg = (A, B, TR, M, MB, K, F, D, C, KC, S, KS, SD, TC, TN, BS)
    dma = pltpu.SemaphoreType.DMA
    hbm = pl.BlockSpec(memory_space=pl.ANY)
    vmem = pl.BlockSpec(memory_space=pltpu.VMEM)
    return pl.pallas_call(
        functools.partial(kernel, cfg),
        out_shape=jax.ShapeDtypeStruct((TR, D), BF),
        in_specs=[hbm, hbm, hbm, vmem, vmem, hbm, vmem],
        out_specs=vmem,
        scratch_shapes=[
            pltpu.VMEM((M, K), BF),
            pltpu.VMEM((S, KS, F), BF),
            pltpu.VMEM((S, KS, F), BF),
            pltpu.VMEM((SD, F, TC), BF),
            pltpu.VMEM((K // BS, F), F32),
            pltpu.VMEM((K // BS, F), F32),
            pltpu.VMEM((F // BS, D), F32),
            pltpu.VMEM((M, F), F32),
            pltpu.VMEM((M, F), F32),
            pltpu.VMEM((NT, 2, M, TN), BF),
            pltpu.VMEM((NT, 2, M, TN), BF),
            pltpu.VMEM((M, F), BF),
            pltpu.VMEM((M, TC), F32),
            pltpu.VMEM((T, M, TC), BF),
            pltpu.VMEM((T, max(B - 1, 1), GR, TC), BF),
            pltpu.VMEM((T, GR, TC), F32),
            pltpu.VMEM((T, GR, TC), BF),
            pltpu.VMEM((T, max(A - 1, 1), TR, TC), BF),
            pltpu.VMEM((T, TR, TC), F32),
            dma((S,)), dma((S,)), dma((SD,)), dma(()),
            dma((C, max(A - 1, 1))), dma((C, max(A - 1, 1))),
            dma((C, max(B - 1, 1), A)), dma((C, max(B - 1, 1), A)),
            dma((NT,)), dma((NT,)),
            dma((T, max(B - 1, 1))), dma((T, max(B - 1, 1))),
            dma((T, max(A - 1, 1))), dma((T, max(A - 1, 1))),
        ],
        compiler_params=pltpu.CompilerParams(
            collective_id=0, has_side_effects=True, vmem_limit_bytes=62 * 2**20
        ),
        cost_estimate=pl.CostEstimate(
            flops=6 * M * K * F, bytes_accessed=6 * K * F, transcendentals=M * F
        ),
    )(tokens, gate_weight, up_weight, gate_mask.T, up_mask.T, down_weight, down_mask)


def solution(mesh):
    in_specs = (
        P(("groups", "blk"), "narrow"),
        P("narrow", "blk"),
        P("narrow", "blk"),
        P("narrow", "blk"),
        P("narrow", "blk"),
        P("blk", "narrow"),
        P("blk", "narrow"),
    )
    out_specs = P(("groups", "blk"), "narrow")
    return jax.shard_map(
        functools.partial(local, mesh.shape["blk"]),
        mesh=mesh, in_specs=in_specs, out_specs=out_specs, check_vma=False,
    )
```
